32 devices in a mesh: dp: 32 (over z, y, x, core).
Axes of the slice: x: 2, y: 2, z: 4, core: 2. Of those that a mesh axis runs over, the one named last changes fastest.
Arguments:
- tokens: bfloat16 [32768, 1024], P('dp'), may hold values from -6 to 6
- ln1_gain: bfloat16 [1024], P('dp'), may hold values from 0.5 to 1.5
- ln1_bias: bfloat16 [1024], P('dp'), may hold values from -1 to 1
- ln2_gain: bfloat16 [1024], P('dp'), may hold values from 0.5 to 1.5
- ln2_bias: bfloat16 [1024], P('dp'), may hold values from -1 to 1
- w_qkv: bfloat16 [1024, 3072], P('dp'), may hold values from -0.1875 to 0.1875
- b_qkv: bfloat16 [3072], P('dp'), may hold values from -1 to 1
- w_dense: bfloat16 [1024, 1024], P('dp'), may hold values from -1.5 to 1.5
- b_dense: bfloat16 [1024], P('dp'), may hold values from -1 to 1
- w_up: bfloat16 [1024, 4096], P('dp'), may hold values from -0.1875 to 0.1875
- b_up: bfloat16 [4096], P('dp'), may hold values from -1 to 1
- w_down: bfloat16 [4096, 1024], P('dp'), may hold values from -0.09375 to 0.09375
- b_down: bfloat16 [1024], P('dp'), may hold values from -1 to 1
- grad_out: bfloat16 [32768, 1024], P('dp'), may hold values from -6 to 6
- seq_lengths: int32 [32, 4], P('dp'), may hold values from 0 to 1024, as said below
Outputs:
- out: bfloat16 [32768, 1024], P('dp')
- grad_tokens: bfloat16 [32768, 1024], P('dp')
- grad_ln1_gain: float32 [1024], P('dp')
- grad_ln1_bias: float32 [1024], P('dp')
- grad_ln2_gain: float32 [1024], P('dp')
- grad_ln2_bias: float32 [1024], P('dp')
- grad_w_qkv: float32 [1024, 3072], P('dp')
- grad_b_qkv: float32 [3072], P('dp')
- grad_w_dense: float32 [1024, 1024], P('dp')
- grad_b_dense: float32 [1024], P('dp')
- grad_w_up: float32 [1024, 4096], P('dp')
- grad_b_up: float32 [4096], P('dp')
- grad_w_down: float32 [4096, 1024], P('dp')
- grad_b_down: float32 [1024], P('dp')
The draws below stay inside these ranges and needn't reach their ends.
Inputs may be any that keep to these rules, and one draw needn't show every extreme that they name: `seq_lengths`: row b lists the lengths of the sequences packed in order into buffer b of 1024 rows; a row sums to 512 or more and to 1024 or less, the remaining rows of the buffer are padding; a zero is an empty slot. In every draw one row, at a place drawn from the seed, holds a single sequence of exactly 1024 tokens.
All inputs are finite; a program needn't handle non-finite values.
Results may differ from the reference program's by a relative error of at most 0.0096.
Values may be sent and summed in bfloat16 or wider, within the bound.
No kernel may reach another device: no remote copies, remote signals or barrier semaphores. Data moves between devices by JAX's collectives and lax.ppermute only.
A program may use at most 256 MiB of HBM per device.

```python
import math
import jax
import jax.numpy as jnp
from jax import lax

D = 1024
HEADS = 16
HD = 64
ROT = 16
FF = 4096
CAP = 1024
SLOTS = 4
BLOCKS = 32
TOKENS = 32768


def draw_seq_lengths(key, part):
    key = jax.random.fold_in(key, 7)
    total_key, cut_key, pick_key = jax.random.split(key, 3)
    totals = jax.random.randint(total_key, (BLOCKS, 1), CAP // 2, CAP + 1).astype(jnp.int32)
    cut_points = jax.random.randint(cut_key, (BLOCKS, SLOTS - 1), 0, totals + 1).astype(jnp.int32)
    cut_points = jnp.sort(cut_points, axis=1)
    boundaries = jnp.concatenate([jnp.zeros((BLOCKS, 1), jnp.int32), cut_points, totals], axis=1)
    lengths = boundaries[:, 1:] - boundaries[:, :-1]
    chosen = jax.random.randint(pick_key, (), 0, BLOCKS)
    whole_row = jnp.concatenate([jnp.full((1,), CAP, jnp.int32), jnp.zeros((SLOTS - 1,), jnp.int32)])
    row_ids = jnp.arange(BLOCKS, dtype=jnp.int32)[:, None]
    return jnp.where(row_ids == chosen, whole_row[None, :], lengths).astype(jnp.int32)


def shard_levels(key, dims, cuts, low, high):
    loudness, own = 1.0, jax.random.fold_in(key, 6)
    for axis_at, parts in cuts:
        heights = jnp.exp(jax.random.uniform(jax.random.fold_in(own, axis_at), (parts,), jnp.float32, low / len(cuts), high / len(cuts)))
        loudness = loudness * jnp.repeat(heights, dims[axis_at] // parts).reshape([-1 if axis == axis_at else 1 for axis in range(len(dims))])
    return loudness


def normal_values(stream_key, dims, deviation, most, cuts=(), held_as=jnp.bfloat16):
    gain = shard_levels(stream_key, dims, cuts, -0.22, 0.18) if cuts else 1.0
    values = jax.random.normal(stream_key, dims, jnp.float32) * deviation * gain
    return jnp.minimum(jnp.maximum(values, -most), most).astype(held_as)


def setup_inputs(seed: int = 0) -> dict:
    arg_keys = jax.random.split(jax.random.key(seed), 16)
    tokens = normal_values(arg_keys[0], (TOKENS, D), 1.0, 6.0, ((0, 32),))
    ln1_gain = jnp.clip(1.0 + 0.1 * jax.random.normal(arg_keys[1], (D,), jnp.float32), 0.5, 1.5).astype(jnp.bfloat16)
    ln1_bias = normal_values(arg_keys[2], (D,), 0.2, 1.0, ((0, 32),))
    ln2_gain = jnp.clip(1.0 + 0.1 * jax.random.normal(arg_keys[3], (D,), jnp.float32), 0.5, 1.5).astype(jnp.bfloat16)
    ln2_bias = normal_values(arg_keys[4], (D,), 0.2, 1.0, ((0, 32),))
    w_qkv = normal_values(arg_keys[5], (D, 3 * D), D ** -0.5, 0.1875, ((0, 32),))
    b_qkv = normal_values(arg_keys[6], (3 * D,), 0.2, 1.0, ((0, 32),))
    w_dense = normal_values(arg_keys[7], (D, D), (D // 64) ** -0.5, 1.5, ((0, 32),))
    b_dense = normal_values(arg_keys[8], (D,), 0.2, 1.0, ((0, 32),))
    w_up = normal_values(arg_keys[9], (D, FF), D ** -0.5, 0.1875, ((0, 32),))
    b_up = normal_values(arg_keys[10], (FF,), 0.2, 1.0, ((0, 32),))
    w_down = normal_values(arg_keys[11], (FF, D), FF ** -0.5, 0.09375, ((0, 32),))
    b_down = normal_values(arg_keys[12], (D,), 0.2, 1.0, ((0, 32),))
    grad_out = normal_values(arg_keys[13], (TOKENS, D), 1.0, 6.0, ((0, 32),))
    seq_lengths = draw_seq_lengths(jax.random.fold_in(arg_keys[15], 71), 0)
    return dict(tokens=tokens, ln1_gain=ln1_gain, ln1_bias=ln1_bias, ln2_gain=ln2_gain, ln2_bias=ln2_bias, w_qkv=w_qkv, b_qkv=b_qkv, w_dense=w_dense, b_dense=b_dense, w_up=w_up, b_up=b_up, w_down=w_down, b_down=b_down, grad_out=grad_out, seq_lengths=seq_lengths)


EPSILON = 1e-05
ROPE_BASE = 10000.0
MASKED = -1e+30
HIGHEST = lax.Precision.HIGHEST

@jax.custom_vjp
def low(v):
    return lax.optimization_barrier(v.astype(jnp.bfloat16)).astype(jnp.float32)

@jax.custom_vjp
def low_back(v):
    return v

def low_keep(v):
    return (low(v), None)

def low_pass(kept, grad):
    return (grad,)

def back_keep(v):
    return (v, None)

def back_low(kept, grad):
    return (low(grad),)
low.defvjp(low_keep, low_pass)
low_back.defvjp(back_keep, back_low)

def layer_norm(values, norm_gain, norm_bias):
    row_mean = lax.optimization_barrier(jnp.mean(values, axis=-1, keepdims=True))
    centered = values - row_mean
    spread = lax.optimization_barrier(jnp.mean(centered * centered, axis=-1, keepdims=True))
    return centered * lax.rsqrt(spread + EPSILON) * norm_gain + norm_bias

def exact_gelu(values):
    return jax.nn.gelu(values, approximate=False)

def token_layout(lengths, row_count):
    seq_ends = jnp.cumsum(lengths).astype(jnp.int32)
    places = jnp.arange(row_count, dtype=jnp.int32)
    passed = seq_ends[None, :] <= places[:, None]
    segment = lax.optimization_barrier(jnp.sum(passed.astype(jnp.int32), axis=1)).astype(jnp.int32)
    seq_start = lax.optimization_barrier(jnp.max(jnp.where(passed, seq_ends[None, :], 0), axis=1)).astype(jnp.int32)
    return (segment, places - seq_start, places < seq_ends[-1])

def rotary_tables(position):
    half_rot = ROT // 2
    exponents = jnp.arange(half_rot, dtype=jnp.float32) * (2.0 / ROT)
    frequency = ROPE_BASE ** (-exponents)
    angles = position.astype(jnp.float32)[:, None] * frequency[None, :]
    angles = jnp.concatenate([angles, angles], axis=-1)
    return (jnp.cos(angles)[:, None, :], jnp.sin(angles)[:, None, :])

def rotate(heads_part, cosines, sines):
    half_rot = ROT // 2
    rotated = heads_part[..., :ROT]
    first_half = rotated[..., :half_rot]
    second_half = rotated[..., half_rot:]
    turned = jnp.concatenate([-second_half, first_half], axis=-1)
    return jnp.concatenate([rotated * cosines + turned * sines, heads_part[..., ROT:]], axis=-1)

def device_forward(stream, lengths, params):
    norm_gain, norm_bias, post_gain, post_bias, qkv_w, qkv_b, dense_w, dense_b, up_w, up_b, down_w, down_b = params
    row_count = stream.shape[0]
    model_width = stream.shape[1]
    query_block = min(512, row_count)
    score_scale = 1.0 / math.sqrt(HD)
    segment, position, is_valid = token_layout(lengths, row_count)
    cosines, sines = rotary_tables(position)
    places = jnp.arange(row_count, dtype=jnp.int32)
    first_in = low(layer_norm(stream, norm_gain, norm_bias))
    projected = low_back(jnp.dot(first_in, qkv_w, precision=HIGHEST) + qkv_b)
    queries = low(rotate(projected[:, :model_width].reshape(row_count, HEADS, HD), cosines, sines))
    keys = low(rotate(projected[:, model_width:2 * model_width].reshape(row_count, HEADS, HD), cosines, sines))
    values = low(projected[:, 2 * model_width:].reshape(row_count, HEADS, HD))

    def attend(block_index):
        row_start = (block_index * query_block).astype(jnp.int32)
        block_q = lax.dynamic_slice_in_dim(queries, row_start, query_block, 0)
        block_seg = lax.dynamic_slice_in_dim(segment, row_start, query_block, 0)
        query_rows = row_start + jnp.arange(query_block, dtype=jnp.int32)
        scores = low_back(jnp.einsum('qhe,khe->hqk', block_q, keys, precision=HIGHEST) * score_scale)
        allowed = (block_seg[:, None] == segment[None, :]) & (places[None, :] <= query_rows[:, None])
        scores = jnp.where(allowed[None], scores, MASKED)
        row_top = lax.optimization_barrier(jnp.max(scores, axis=-1, keepdims=True))
        weights = jnp.exp(scores - row_top)
        weights_low = low(weights / lax.optimization_barrier(jnp.sum(weights, axis=-1, keepdims=True)))
        return jnp.einsum('hqk,khe->qhe', weights_low, values, precision=HIGHEST)
    mixed_heads = lax.map(jax.checkpoint(attend), jnp.arange(row_count // query_block, dtype=jnp.int32))
    mixed_low = low(low_back(mixed_heads.reshape(row_count, model_width)))
    attention_out = jnp.dot(mixed_low, dense_w, precision=HIGHEST) + dense_b
    second_in = low(layer_norm(stream, post_gain, post_bias))
    hidden_pre = low_back(jnp.dot(second_in, up_w, precision=HIGHEST) + up_b)
    active = low(exact_gelu(hidden_pre))
    feed_out = jnp.dot(active, down_w, precision=HIGHEST) + down_b
    return stream + attention_out + feed_out

def reference(tokens, ln1_gain, ln1_bias, ln2_gain, ln2_bias, w_qkv, b_qkv, w_dense, b_dense, w_up, b_up, w_down, b_down, grad_out, seq_lengths):
    params = tuple((weight_arg.astype(jnp.float32) for weight_arg in (ln1_gain, ln1_bias, ln2_gain, ln2_bias, w_qkv, b_qkv, w_dense, b_dense, w_up, b_up, w_down, b_down)))
    stream = tokens.astype(jnp.float32).reshape(BLOCKS, CAP, D)

    def forward(stream_in, params_in):

        def one_device(device_item):
            return device_forward(device_item[0], device_item[1], params_in)
        return lax.map(jax.checkpoint(one_device), (stream_in, seq_lengths))
    result, pull_back = jax.vjp(forward, stream, params)

    def valid_rows(lengths):
        return token_layout(lengths, CAP)[2].astype(jnp.float32)
    is_valid = lax.map(valid_rows, seq_lengths)
    cotangent = grad_out.astype(jnp.float32).reshape(BLOCKS, CAP, D) * is_valid[..., None]
    grad_stream, grads = pull_back(cotangent)
    return (result.reshape(TOKENS, D).astype(jnp.bfloat16), grad_stream.reshape(TOKENS, D).astype(jnp.bfloat16), grads[0], grads[1], grads[2], grads[3], grads[4], grads[5], grads[6], grads[7], grads[8], grads[9], grads[10], grads[11])
```

```python
import functools
import math

import jax
import jax.numpy as jnp
from jax import lax
from jax.experimental import pallas as pl
from jax.experimental.pallas import tpu as pltpu
from jax.sharding import PartitionSpec as P

HEADS = 16
ROT = 16
EPSILON = 1e-05
ROPE_BASE = 10000.0
MASKED = -1e30
VMEM_LIMIT = 56 * 1024 * 1024

ERF_P = 0.38
ERF_C = (
    0.2144098448037192,
    0.21394421331748759,
    0.20368721918248728,
    0.13967175645997887,
    0.22724170102679003,
    -0.15687572740913802,
    0.3593738707984917,
    -0.25987872992383027,
    0.05842583978543742,
)


def gelu_pair(pre):
    size = jnp.abs(pre)
    bell = jnp.exp(pre * pre * -0.5)
    t = pltpu.reciprocal(size * (ERF_P / math.sqrt(2.0)) + 1.0, approx=False)
    poly = jnp.full_like(t, 0.5 * ERF_C[-1])
    for coef in ERF_C[-2::-1]:
        poly = poly * t + 0.5 * coef
    tail = poly * t * bell
    cdf = jnp.where(pre < 0.0, tail, 1.0 - tail)
    return pre * cdf, cdf + pre * bell * (1.0 / math.sqrt(2.0 * math.pi))


def nt(a, b):
    return lax.dot_general(a, b, (((1,), (1,)), ((), ())), preferred_element_type=jnp.float32)


def nn(a, b):
    return jnp.dot(a, b, preferred_element_type=jnp.float32)


def feed_kernel(rows, own, me_ref, h_ref, dy_ref, up_ref, bias_ref, down_ref, *refs):
    act_ref, low_ref, high_ref, dpre_ref, dbias_ref = refs[-5:]
    total, model = h_ref.shape
    block = 8 * own
    up = up_ref[...].reshape(model, block)
    down = down_ref[...].reshape(block, model)
    me = me_ref[0]
    mine = (me & 1) == 0
    spots = []
    for x in range(2):
        for y in range(2):
            far_x = ((me >> 1) & 1) ^ x
            far_y = ((me >> 2) & 1) ^ y
            even = far_x * 2 + far_y
            odd = far_y * 2 + far_x
            low = pl.ds(pl.multiple_of(jnp.where(mine, even, odd) * own, own), own)
            high = pl.ds(pl.multiple_of(jnp.where(mine, odd, even) * own, own), own)
            spots.append(((y * 4 + x * 2) * own, low, high))
    sums = jnp.zeros((1, block), jnp.float32)
    for start in range(0, total, rows):
        part = pl.ds(start, rows)
        pre = nn(h_ref[part, :], up) + bias_ref[...]
        dact = nt(dy_ref[part, :], down)
        act, slope = gelu_pair(pre)
        act = act.astype(jnp.bfloat16)
        act_ref[part, :] = act
        dpre = (dact * slope).astype(jnp.bfloat16)
        dpre_ref[part, :] = dpre
        sums = sums + jnp.sum(dpre.astype(jnp.float32), axis=0, keepdims=True)
        for at, low, high in spots:
            even, odd = act[:, at : at + own], act[:, at + own : at + 2 * own]
            low_ref[part, low] = jnp.where(mine, even, odd)
            high_ref[part, high] = jnp.where(mine, odd, even)
    dbias_ref[...] = sums


def feed_specs(count, model, own, depth, devices):
    pieces = 8 * own // model
    up = pl.BlockSpec((devices, pieces, depth, model), lambda i, *me: (0, i, 0, 0))
    span = own // depth
    down = pl.BlockSpec((8, span, depth, model), lambda i, *me: (i, 1, 0, 0))
    return up, down


def feed_forward(me, h, dy, weights, bias, own, after, rows=256):
    count, model = h.shape
    devices, depth = weights.shape[0], weights.shape[2]
    hidden = devices * own
    block = 8 * own
    whole = pl.BlockSpec((count, model), lambda i, me: (0, 0))
    wide = pl.BlockSpec((count, block), lambda i, me: (0, i))
    half = pl.BlockSpec((count, block // 2), lambda i, me: (0, i ^ (me[0] >> 3)))
    line = pl.BlockSpec((1, block), lambda i, me: (0, i))
    whole_shape = jax.ShapeDtypeStruct((count, hidden), jnp.bfloat16)
    half_shape = jax.ShapeDtypeStruct((count, hidden // 2), jnp.bfloat16)
    up, down = feed_specs(count, model, own, depth, devices)
    return pl.pallas_call(
        functools.partial(feed_kernel, min(rows, count), own),
        grid_spec=pltpu.PrefetchScalarGridSpec(
            num_scalar_prefetch=1,
            grid=(hidden // block,),
            in_specs=[whole, whole, up, line, down] + [pl.BlockSpec(memory_space=pl.ANY)] * len(after),
            out_specs=[wide, half, half, wide, line],
        ),
        out_shape=[whole_shape, half_shape, half_shape, whole_shape, jax.ShapeDtypeStruct((1, hidden), jnp.float32)],
        compiler_params=pltpu.CompilerParams(vmem_limit_bytes=VMEM_LIMIT),
        cost_estimate=pl.CostEstimate(
            flops=4 * count * model * hidden,
            bytes_accessed=4 * count * model + 4 * model * hidden + 6 * count * hidden,
            transcendentals=2 * count * hidden,
        ),
        name="feed_forward",
    )(me, h, dy, weights, bias, weights, *after)


def close_kernel(rows, own, rule, left_ref, right_ref, *refs):
    out_ref = refs[-1]
    total, model = out_ref.shape
    block = 8 * own
    right = right_ref[...].reshape((model, block) if rule is nt else (block, model))

    @pl.when(pl.program_id(0) == 0)
    def _():
        out_ref[...] = jnp.zeros_like(out_ref)

    for start in range(0, total, rows):
        part = pl.ds(start, rows)
        out_ref[part, :] += rule(left_ref[part, :], right)


def feed_close(left, weights, own, rule, after, rows=256):
    count, hidden = left.shape
    devices, depth, model = weights.shape[0], weights.shape[2], weights.shape[3]
    wide = pl.BlockSpec((count, 8 * own), lambda i: (0, i))
    whole = pl.BlockSpec((count, model), lambda i: (0, 0))
    up, down = feed_specs(count, model, own, depth, devices)
    return pl.pallas_call(
        functools.partial(close_kernel, min(rows, count), own, rule),
        grid=(hidden // (8 * own),),
        in_specs=[wide, up if rule is nt else down] + [pl.BlockSpec(memory_space=pl.ANY)] * len(after),
        out_specs=whole,
        out_shape=jax.ShapeDtypeStruct((count, model), jnp.float32),
        compiler_params=pltpu.CompilerParams(vmem_limit_bytes=VMEM_LIMIT),
        cost_estimate=pl.CostEstimate(
            flops=2 * count * model * hidden,
            bytes_accessed=4 * count * model + 2 * model * hidden + 2 * count * hidden,
            transcendentals=0,
        ),
        name="feed_close",
    )(left, weights, *after)


def turn(x, cosines, sines, head):
    half = ROT // 2
    parts = []
    for start in range(0, x.shape[0], head):
        first = x[start : start + half]
        second = x[start + half : start + ROT]
        parts.append(first * cosines - second * sines)
        parts.append(second * cosines + first * sines)
        parts.append(x[start + ROT : start + head])
    return jnp.concatenate(parts, axis=0)


def attention_kernel(
    block, head, q_ref, k_ref, v_ref, g_ref, cos_ref, sin_ref, start_ref, mixed_ref, grad_ref, dk_ref, dv_ref
):
    width, count = q_ref.shape
    cosines = cos_ref[...]
    sines = sin_ref[...]
    queries = turn(q_ref[...], cosines, sines, head).astype(jnp.bfloat16) * jnp.bfloat16(1.0 / math.sqrt(head))
    keys = turn(k_ref[...], cosines, sines, head).astype(jnp.bfloat16)
    values = v_ref[...].astype(jnp.bfloat16)
    grads = g_ref[...]
    keys_t = keys.T
    values_t = values.T
    row_of = lax.broadcasted_iota(jnp.int32, (width, 1), 0) // head
    lane_of = lax.broadcasted_iota(jnp.int32, (1, width), 1) // head
    dk_ref[...] = jnp.zeros_like(dk_ref)
    dv_ref[...] = jnp.zeros_like(dv_ref)
    for low in range(0, count, block):
        high = low + block
        seq_start = start_ref[:, low:high]
        key_at = lax.broadcasted_iota(jnp.int32, (high, block), 0)
        query_at = lax.broadcasted_iota(jnp.int32, (high, block), 1) + low
        allowed = (key_at >= seq_start) & (key_at <= query_at)
        q_block = queries[:, low:high]
        g_block = grads[:, low:high]
        q_back = q_block.T
        g_back = g_block.T
        mixed_parts = []
        dq_parts = []
        for at in range(width // head):
            rows = slice(at * head, (at + 1) * head)
            mine = row_of == at
            q_own = jnp.where(mine, q_block, jnp.bfloat16(0))
            g_own = jnp.where(mine, g_block, jnp.bfloat16(0))
            scores = nn(keys_t[:high], q_own)
            scores = jnp.where(allowed, scores, MASKED)
            top = jnp.max(scores, axis=0, keepdims=True)
            weights = jnp.exp(scores - top)
            weights = weights * (1.0 / jnp.sum(weights, axis=0, keepdims=True))
            weights_low = weights.astype(jnp.bfloat16)
            mixed_parts.append(nn(values[rows, :high], weights_low))
            dweights = nn(values_t[:high], g_own)
            delta = jnp.sum(weights * dweights, axis=0, keepdims=True)
            dscores = (weights * (dweights - delta)).astype(jnp.bfloat16)
            dq_parts.append(nn(keys[rows, :high], dscores))
            own_lane = lane_of == at
            dk_ref[:high, :] += nn(dscores, jnp.where(own_lane, q_back, jnp.bfloat16(0)))
            dv_ref[:high, :] += nn(weights_low, jnp.where(own_lane, g_back, jnp.bfloat16(0)))
        mixed_ref[:, low:high] = jnp.concatenate(mixed_parts, axis=0).astype(jnp.bfloat16)
        dq = jnp.concatenate(dq_parts, axis=0) * (1.0 / math.sqrt(head))
        grad_ref[0, :, low:high] = turn(dq, cosines[:, low:high], -sines[:, low:high], head).astype(jnp.bfloat16)
    grad_ref[1] = turn(dk_ref[...].T, cosines, -sines, head).astype(jnp.bfloat16)
    grad_ref[2] = dv_ref[...].T.astype(jnp.bfloat16)


def attention(projected_t, dmixed_t, cosines, sines, seq_start, block=512):
    model, count = dmixed_t.shape
    head = model // HEADS
    width = 2 * head
    steps = model // width
    block = min(block, count)
    return pl.pallas_call(
        functools.partial(attention_kernel, block, head),
        grid=(steps,),
        in_specs=[
            pl.BlockSpec((width, count), lambda i: (i, 0)),
            pl.BlockSpec((width, count), lambda i: (i + steps, 0)),
            pl.BlockSpec((width, count), lambda i: (i + 2 * steps, 0)),
            pl.BlockSpec((width, count), lambda i: (i, 0)),
            pl.BlockSpec((ROT // 2, count), lambda i: (0, 0)),
            pl.BlockSpec((ROT // 2, count), lambda i: (0, 0)),
            pl.BlockSpec((1, count), lambda i: (0, 0)),
        ],
        out_specs=[
            pl.BlockSpec((width, count), lambda i: (i, 0)),
            pl.BlockSpec((3, width, count), lambda i: (0, i, 0)),
        ],
        out_shape=[
            jax.ShapeDtypeStruct((model, count), jnp.bfloat16),
            jax.ShapeDtypeStruct((3, model, count), jnp.bfloat16),
        ],
        scratch_shapes=[pltpu.VMEM((count, width), jnp.float32), pltpu.VMEM((count, width), jnp.float32)],
        compiler_params=pltpu.CompilerParams(vmem_limit_bytes=VMEM_LIMIT),
        cost_estimate=pl.CostEstimate(
            flops=12 * count * count * model,
            bytes_accessed=22 * count * model,
            transcendentals=count * count * HEADS // 2,
        ),
        name="attention",
    )(projected_t, projected_t, projected_t, dmixed_t, cosines, sines, seq_start)


def link_bits(count):
    size = count.bit_length() - 1
    top = list(range(size - 1, 2, -1))
    if size < 3:
        return [list(range(size - 1, 0, -1))] * 2
    return [top + [1, 2], top + [2, 1]]


def relative_blocks(count):
    by_core = link_bits(count)
    half = count // 2
    tables = []
    for core in range(2):
        places = []
        for place in range(count):
            other = place // half
            bits = by_core[core ^ other]
            distance = other
            for at, bit in enumerate(bits):
                if (place >> (len(bits) - 1 - at)) & 1:
                    distance |= 1 << bit
            places.append(distance)
        tables.append(places)
    return tables


def core_pairs(count):
    return [(i, i ^ 1) for i in range(count)]


def link_pairs(count, axis):
    by_core = link_bits(count)
    return [(i, i ^ (1 << by_core[i & 1][axis])) for i in range(count)]


class Halving:
    def __init__(self, count, blocks, order, exact=False):
        size = count.bit_length() - 2
        self.count = count
        self.buf = blocks.reshape((2,) * size + blocks.shape[1:])
        self.left = list(range(size))
        self.order = list(order)
        self.exact = exact

    def step(self, *fences):
        stage = self.order.pop(0)
        axis = self.left.index(stage)
        self.left.remove(stage)
        sent = lax.index_in_dim(self.buf, 1, axis, keepdims=False)
        kept = lax.index_in_dim(self.buf, 0, axis, keepdims=False)
        got = lax.ppermute(sent, "dp", link_pairs(self.count, stage))
        total = kept.astype(jnp.float32) + got.astype(jnp.float32) + nothing(*fences)
        self.buf = total.astype(jnp.bfloat16) if self.left and not self.exact else total

    def finish(self):
        while self.order:
            self.step()
        return self.buf


def orders(count):
    size = count.bit_length() - 2
    if size < 3:
        return list(range(size)), list(range(size))[::-1]
    top = list(range(size - 2))
    plane = [size - 2, size - 1]
    return plane + top[::-1], [top[-1]] + plane + top[-2::-1]


def collect(count, own, order):
    size = count.bit_length() - 2
    buf = own.reshape((1,) * size + own.shape)
    for stage in order[::-1]:
        got = lax.ppermute(buf, "dp", link_pairs(count, stage))
        buf = jnp.concatenate([buf, got], axis=stage)
    low = buf.reshape((count // 2,) + own.shape)
    return low, lax.ppermute(low, "dp", core_pairs(count))


def nothing(*values):
    total = 0.0
    for value in values:
        total = total + value[(0,) * value.ndim].astype(jnp.float32) * 0.0
    return total


def later(shard, *values):
    return (shard.astype(jnp.float32) + nothing(*values)).astype(shard.dtype)


def tn(a, b):
    return lax.dot_general(a, b, (((0,), (0,)), ((), ())), preferred_element_type=jnp.float32)


def norm_parts(stream):
    row_mean = jnp.mean(stream, axis=-1, keepdims=True)
    centered = stream - row_mean
    spread = jnp.mean(centered * centered, axis=-1, keepdims=True)
    factor = lax.rsqrt(spread + EPSILON)
    return centered * factor, factor


def shards(
    tokens,
    ln1_gain,
    ln1_bias,
    ln2_gain,
    ln2_bias,
    w_qkv,
    b_qkv,
    w_dense,
    b_dense,
    w_up,
    b_up,
    w_down,
    b_down,
    grad_out,
    seq_lengths,
    count,
):
    f32 = jnp.float32
    bf16 = jnp.bfloat16
    rows, model = tokens.shape
    depth = w_up.shape[0]
    own_hidden = w_down.shape[0]
    hidden = count * own_hidden
    me = lax.axis_index("dp").astype(jnp.int32)
    small = [ln1_gain, ln1_bias, ln2_gain, ln2_bias, b_qkv, b_dense, b_up, b_down]
    lanes = 128 * (-(-max(v.shape[0] for v in small) // 128))
    small_rows = jnp.stack([jnp.pad(v, (0, lanes - v.shape[0])) for v in small])
    order_a, order_b = orders(count)
    tables = jnp.asarray(relative_blocks(count), jnp.int32)
    block_at = me ^ tables[me & 1]
    small_low, small_high = collect(count, small_rows, order_a)
    smalls = jnp.concatenate([small_low, small_high], axis=0)
    back = jnp.argsort(block_at)
    smalls = jnp.take(smalls, back, axis=0).astype(f32)
    gain1, bias1, gain2, bias2, qkv_b, dense_b, up_b, down_b = (
        smalls[:, at, : v.shape[0]].reshape(1, count * v.shape[0]) for at, v in enumerate(small)
    )
    attention_w = lax.all_gather(jnp.concatenate([w_qkv, w_dense], axis=1), "dp", axis=0, tiled=True)
    qkv_w, dense_w = attention_w[:, : 3 * model], attention_w[:, 3 * model :]

    seq_ends = jnp.cumsum(seq_lengths[0])
    places = jnp.arange(rows, dtype=jnp.int32)
    passed = seq_ends[None, :] <= places[:, None]
    seq_start = jnp.max(jnp.where(passed, seq_ends[None, :], 0), axis=1)
    is_valid = places < seq_ends[-1]
    half_rot = ROT // 2
    frequency = ROPE_BASE ** (-(jnp.arange(half_rot, dtype=f32) * (2.0 / ROT)))
    angles = frequency[:, None] * (places - seq_start).astype(f32)[None, :]
    cosines, sines = jnp.cos(angles), jnp.sin(angles)

    stream = tokens.astype(f32)
    normed, factor = norm_parts(stream)
    first_in = (normed * gain1 + bias1).astype(bf16)
    second_in = (normed * gain2 + bias2).astype(bf16)
    grad_y = grad_out * is_valid.astype(bf16)[:, None]

    row_at = (block_at[:, None] * depth + jnp.arange(depth, dtype=jnp.int32)[None, :]).reshape(model, 1)
    place = (row_at == jnp.arange(model, dtype=jnp.int32)[None, :]).astype(bf16)
    out_bias = jnp.sum(grad_y.astype(f32), axis=0)
    first_t = nt(place, first_in).astype(bf16)
    second_t = nt(place, second_in).astype(bf16)

    grouped = own_hidden % 128 == 0 and count >= 8 and (8 * own_hidden) == model and own_hidden % depth == 0
    if grouped:
        pieces = hidden // model
        stacked_w = jnp.concatenate(
            [w_up[:, at * model : (at + 1) * model] for at in range(pieces)] + [w_down], axis=0
        )
        feed_w = lax.all_gather(later(stacked_w, attention_w, first_t, second_t, cosines, sines, out_bias), "dp", axis=0, tiled=True)
        feed_w = feed_w.reshape(count, -1, depth, model)
    else:
        up_w = lax.all_gather(later(w_up, attention_w), "dp", axis=0, tiled=True)
        down_w = lax.all_gather(later(w_down, up_w), "dp", axis=0, tiled=True)

    def exchange(upper, lower, rhs, rule, *fences):
        sent = (rule(upper, rhs) + nothing(*fences)).astype(bf16)
        got = lax.ppermute(sent, "dp", core_pairs(count))
        kept = (rule(lower, rhs) + got.astype(f32)).astype(bf16)
        return kept.reshape(count // 2, kept.shape[0] * 2 // count, -1)

    half = model // 2
    projected_t = lax.dot_general(qkv_w, first_in, (((0,), (1,)), ((), ())), preferred_element_type=f32)
    projected_t = projected_t + qkv_b.reshape(-1, 1)
    dmixed_t = nt(dense_w, grad_y).astype(bf16)
    mixed_t, grads_t = attention(projected_t, dmixed_t, cosines, sines, seq_start.reshape(1, rows))
    grads_t = grads_t.reshape(3 * model, rows)
    mixed_p = nn(place, mixed_t).astype(bf16)
    qkv_kept = exchange(first_t[half:], first_t[:half], grads_t, nt)
    dense_kept = exchange(mixed_p[half:], mixed_p[:half], grad_y, nn)
    qkv_sum = Halving(count, qkv_kept, order_a)
    dense_sum = Halving(count, dense_kept, order_b)
    if grouped:
        act, act_low, act_high, dpre, up_sums = feed_forward(
            me.reshape(1), second_in, grad_y, feed_w, up_b, own_hidden, (qkv_kept, dense_kept)
        )
    else:
        act, slope = gelu_pair(nn(second_in, up_w) + up_b)
        act = act.astype(bf16)
        act_p = jnp.take(act.reshape(rows, count, own_hidden), block_at, axis=1).reshape(rows, hidden)
        act_low, act_high = act_p[:, : hidden // 2], act_p[:, hidden // 2 :]
        dpre = (nt(grad_y, down_w) * slope).astype(bf16)
        up_sums = jnp.sum(dpre.astype(f32), axis=0)
    qkv_sum.step(dpre)
    dense_sum.step(dpre)
    down_kept = exchange(act_high, act_low, grad_y, tn, qkv_sum.buf, dense_sum.buf)
    qkv_sum.step(down_kept)
    dense_sum.step(down_kept)
    down_sum = Halving(count, down_kept, order_a)
    up_kept = exchange(second_t[half:], second_t[:half], dpre, nn, qkv_sum.buf, dense_sum.buf)
    up_sum = Halving(count, up_kept, order_a)
    down_sum.step(up_kept)
    qkv_sum.step(up_kept)
    dense_sum.step(up_kept)

    if grouped:
        after = (up_kept, down_sum.buf, qkv_sum.buf, dense_sum.buf)
        grad_second = feed_close(dpre, feed_w, own_hidden, nt, after)
    else:
        grad_second = nt(dpre, up_w)
    grad_first = lax.dot_general(grads_t, qkv_w, (((0,), (1,)), ((), ())), preferred_element_type=f32)
    grad_first = grad_first + nothing(down_sum.buf)
    for chain in (down_sum, up_sum, qkv_sum, dense_sum):
        chain.step(grad_second, grad_first)
    qkv_part = qkv_sum.finish()
    dense_part = dense_sum.finish()

    pull = grad_first * gain1 + grad_second * gain2
    pull_mean = jnp.mean(pull, axis=-1, keepdims=True)
    pull_norm = jnp.mean(pull * normed, axis=-1, keepdims=True)
    grad_x = factor * (pull - pull_mean - normed * pull_norm)
    grad_tokens = (grad_y.astype(f32) + grad_x).astype(bf16)
    small_grads = [
        jnp.sum(grad_first * normed, axis=0),
        jnp.sum(grad_first, axis=0),
        jnp.sum(grad_second * normed, axis=0),
        jnp.sum(grad_second, axis=0),
        jnp.sum(grads_t.astype(f32), axis=1),
        out_bias,
        up_sums.reshape(-1),
    ]
    stacked = jnp.concatenate([v.reshape(count, -1) for v in small_grads], axis=1)
    stacked = jnp.take(stacked, block_at, axis=0) + nothing(down_sum.buf, up_sum.buf)
    middle = count // 2
    buf = stacked[:middle] + lax.ppermute(stacked[middle:], "dp", core_pairs(count))
    small_sum = Halving(count, buf.reshape(middle, 1, -1), order_a, exact=True)
    if grouped:
        feed_out = feed_close(act, feed_w, own_hidden, nn, (down_sum.buf, up_sum.buf))
    else:
        feed_out = nn(act, down_w)
    attention_out = lax.dot_general(mixed_t, dense_w, (((0,), (0,)), ((), ())), preferred_element_type=f32)
    down_sum.step(feed_out)
    up_sum.step(feed_out)
    result = (stream + attention_out + dense_b + feed_out + down_b + nothing(up_sum.buf)).astype(bf16)
    if up_sum.order:
        up_sum.step(result)
    if down_sum.order:
        down_sum.step(result)
    down_part = down_sum.finish()
    up_part = up_sum.finish()
    buf = small_sum.finish()
    small_out = []
    at = 0
    for v in small_grads:
        size = v.shape[0] // count
        small_out.append(buf[0, at : at + size])
        at += size
    gain1_part, bias1_part, gain2_part, bias2_part, qkv_bias_part, out_bias_part, up_bias_part = small_out
    return (
        result,
        grad_tokens,
        gain1_part,
        bias1_part,
        gain2_part,
        bias2_part,
        qkv_part,
        qkv_bias_part,
        dense_part,
        out_bias_part,
        up_part,
        up_bias_part,
        down_part,
        out_bias_part,
    )


def solution(mesh):
    count = mesh.shape["dp"]
    row, flat = P("dp", None), P("dp")
    in_specs = (row, flat, flat, flat, flat, row, flat, row, flat, row, flat, row, flat, row, row)
    out_specs = (row, row, flat, flat, flat, flat, row, flat, row, flat, row, flat, row, flat)
    return jax.shard_map(
        functools.partial(shards, count=count), mesh=mesh, in_specs=in_specs, out_specs=out_specs, check_vma=False
    )
```

```python
import functools
import math

import jax
import jax.numpy as jnp
from jax import lax
from jax.experimental import pallas as pl
from jax.experimental.pallas import tpu as pltpu
from jax.sharding import PartitionSpec as P

HEADS = 16
ROT = 16
EPSILON = 1e-05
ROPE_BASE = 10000.0
MASKED = -1e30
VMEM_LIMIT = 56 * 1024 * 1024

ERF_P = 0.38
ERF_C = (
    0.2144098448037192,
    0.21394421331748759,
    0.20368721918248728,
    0.13967175645997887,
    0.22724170102679003,
    -0.15687572740913802,
    0.3593738707984917,
    -0.25987872992383027,
    0.05842583978543742,
)


def gelu_pair(pre):
    size = jnp.abs(pre)
    bell = jnp.exp(pre * pre * -0.5)
    t = pltpu.reciprocal(size * (ERF_P / math.sqrt(2.0)) + 1.0, approx=False)
    poly = jnp.full_like(t, 0.5 * ERF_C[-1])
    for coef in ERF_C[-2::-1]:
        poly = poly * t + 0.5 * coef
    tail = poly * t * bell
    cdf = jnp.where(pre < 0.0, tail, 1.0 - tail)
    return pre * cdf, cdf + pre * bell * (1.0 / math.sqrt(2.0 * math.pi))


def nt(a, b):
    return lax.dot_general(a, b, (((1,), (1,)), ((), ())), preferred_element_type=jnp.float32)


def nn(a, b):
    return jnp.dot(a, b, preferred_element_type=jnp.float32)


def feed_kernel(rows, own, me_ref, h_ref, dy_ref, up_ref, bias_ref, down_ref, *refs):
    act_ref, halves_ref, dpre_ref, dbias_ref = refs[-4:]
    total, model = h_ref.shape
    block = 8 * own
    up = up_ref[...].reshape(model, block)
    down = down_ref[...].reshape(block, model)
    me = me_ref[0]
    core = me & 1
    spots = []
    for x in range(2):
        for y in range(2):
            far_x = ((me >> 1) & 1) ^ x
            far_y = ((me >> 2) & 1) ^ y
            x_lane = pl.ds(pl.multiple_of(far_x * own, own), own)
            y_lane = pl.ds(pl.multiple_of(far_y * own, own), own)
            spots.append(((y * 4 + x * 2) * own, far_x, x_lane, far_y, y_lane))
    sums = jnp.zeros((1, block), jnp.float32)
    for start in range(0, total, rows):
        part = pl.ds(start, rows)
        pre = nn(h_ref[part, :], up) + bias_ref[...]
        dact = nt(dy_ref[part, :], down)
        act, slope = gelu_pair(pre)
        act = act.astype(jnp.bfloat16)
        act_ref[part, :] = act
        dpre = (dact * slope).astype(jnp.bfloat16)
        dpre_ref[part, :] = dpre
        sums = sums + jnp.sum(dpre.astype(jnp.float32), axis=0, keepdims=True)
        for at, far_x, x_lane, far_y, y_lane in spots:
            halves_ref[core, far_x, part, y_lane] = act[:, at : at + own]
            halves_ref[1 - core, far_y, part, x_lane] = act[:, at + own : at + 2 * own]
    dbias_ref[...] = sums


def feed_specs(count, model, own, depth, devices):
    pieces = 8 * own // model
    up = pl.BlockSpec((devices, pieces, depth, model), lambda i, *me: (0, i, 0, 0))
    span = own // depth
    down = pl.BlockSpec((8, span, depth, model), lambda i, *me: (i, 1, 0, 0))
    return up, down


def feed_forward(me, h, dy, weights, bias, own, after, rows=256):
    count, model = h.shape
    devices, depth = weights.shape[0], weights.shape[2]
    hidden = devices * own
    block = 8 * own
    whole = pl.BlockSpec((count, model), lambda i, me: (0, 0))
    wide = pl.BlockSpec((count, block), lambda i, me: (0, i))
    halves = pl.BlockSpec((2, 2, count, block // 4), lambda i, me: (0, 0, 0, i ^ (me[0] >> 3)))
    line = pl.BlockSpec((1, block), lambda i, me: (0, i))
    whole_shape = jax.ShapeDtypeStruct((count, hidden), jnp.bfloat16)
    halves_shape = jax.ShapeDtypeStruct((2, 2, count, hidden // 4), jnp.bfloat16)
    up, down = feed_specs(count, model, own, depth, devices)
    return pl.pallas_call(
        functools.partial(feed_kernel, min(rows, count), own),
        grid_spec=pltpu.PrefetchScalarGridSpec(
            num_scalar_prefetch=1,
            grid=(hidden // block,),
            in_specs=[whole, whole, up, line, down] + [pl.BlockSpec(memory_space=pl.ANY)] * len(after),
            out_specs=[wide, halves, wide, line],
        ),
        out_shape=[whole_shape, halves_shape, whole_shape, jax.ShapeDtypeStruct((1, hidden), jnp.float32)],
        compiler_params=pltpu.CompilerParams(vmem_limit_bytes=VMEM_LIMIT),
        cost_estimate=pl.CostEstimate(
            flops=4 * count * model * hidden,
            bytes_accessed=4 * count * model + 4 * model * hidden + 6 * count * hidden,
            transcendentals=2 * count * hidden,
        ),
        name="feed_forward",
    )(me, h, dy, weights, bias, weights, *after)


def close_kernel(rows, own, rule, left_ref, right_ref, *refs):
    out_ref = refs[-1]
    total, model = out_ref.shape
    block = 8 * own
    right = right_ref[...].reshape((model, block) if rule is nt else (block, model))

    @pl.when(pl.program_id(0) == 0)
    def _():
        out_ref[...] = jnp.zeros_like(out_ref)

    for start in range(0, total, rows):
        part = pl.ds(start, rows)
        out_ref[part, :] += rule(left_ref[part, :], right)


def feed_close(left, weights, own, rule, after, rows=256):
    count, hidden = left.shape
    devices, depth, model = weights.shape[0], weights.shape[2], weights.shape[3]
    wide = pl.BlockSpec((count, 8 * own), lambda i: (0, i))
    whole = pl.BlockSpec((count, model), lambda i: (0, 0))
    up, down = feed_specs(count, model, own, depth, devices)
    return pl.pallas_call(
        functools.partial(close_kernel, min(rows, count), own, rule),
        grid=(hidden // (8 * own),),
        in_specs=[wide, up if rule is nt else down] + [pl.BlockSpec(memory_space=pl.ANY)] * len(after),
        out_specs=whole,
        out_shape=jax.ShapeDtypeStruct((count, model), jnp.float32),
        compiler_params=pltpu.CompilerParams(vmem_limit_bytes=VMEM_LIMIT),
        cost_estimate=pl.CostEstimate(
            flops=2 * count * model * hidden,
            bytes_accessed=4 * count * model + 2 * model * hidden + 2 * count * hidden,
            transcendentals=0,
        ),
        name="feed_close",
    )(left, weights, *after)


def combine_kernel(kept_ref, got_ref, *refs):
    sent_ref, left_ref = refs[-2:]
    total = kept_ref[0].astype(jnp.float32) + got_ref[0].astype(jnp.float32)
    total = total.astype(jnp.bfloat16)
    left_ref[0] = total[0]
    sent_ref[0] = total[1]


def combine(kept, got, after):
    places, rows, columns = got.shape
    pair = pl.BlockSpec((1, 2, rows, columns), lambda i: (i, 0, 0, 0))
    one = pl.BlockSpec((1, rows, columns), lambda i: (i, 0, 0))
    shape = jax.ShapeDtypeStruct((places // 2, rows, columns), jnp.bfloat16)
    paired = (-1, 2, rows, columns)
    return pl.pallas_call(
        combine_kernel,
        grid=(places // 2,),
        in_specs=[pair, pair] + [pl.BlockSpec(memory_space=pl.ANY)] * len(after),
        out_specs=[one, one],
        out_shape=[shape, shape],
        compiler_params=pltpu.CompilerParams(vmem_limit_bytes=VMEM_LIMIT),
        cost_estimate=pl.CostEstimate(
            flops=places * rows * columns, bytes_accessed=6 * places * rows * columns, transcendentals=0
        ),
        name="combine",
    )(kept.reshape(paired), got.reshape(paired), *after)


def turn(x, cosines, sines, head):
    half = ROT // 2
    parts = []
    for start in range(0, x.shape[0], head):
        first = x[start : start + half]
        second = x[start + half : start + ROT]
        parts.append(first * cosines - second * sines)
        parts.append(second * cosines + first * sines)
        parts.append(x[start + ROT : start + head])
    return jnp.concatenate(parts, axis=0)


def attention_kernel(
    block, head, q_ref, k_ref, v_ref, g_ref, cos_ref, sin_ref, start_ref, mixed_ref, grad_ref, dk_ref, dv_ref
):
    width, count = q_ref.shape
    cosines = cos_ref[...]
    sines = sin_ref[...]
    queries = turn(q_ref[...], cosines, sines, head).astype(jnp.bfloat16) * jnp.bfloat16(1.0 / math.sqrt(head))
    keys = turn(k_ref[...], cosines, sines, head).astype(jnp.bfloat16)
    values = v_ref[...].astype(jnp.bfloat16)
    grads = g_ref[...]
    keys_t = keys.T
    values_t = values.T
    row_of = lax.broadcasted_iota(jnp.int32, (width, 1), 0) // head
    lane_of = lax.broadcasted_iota(jnp.int32, (1, width), 1) // head
    dk_ref[...] = jnp.zeros_like(dk_ref)
    dv_ref[...] = jnp.zeros_like(dv_ref)
    for low in range(0, count, block):
        high = low + block
        seq_start = start_ref[:, low:high]
        key_at = lax.broadcasted_iota(jnp.int32, (high, block), 0)
        query_at = lax.broadcasted_iota(jnp.int32, (high, block), 1) + low
        allowed = (key_at >= seq_start) & (key_at <= query_at)
        q_block = queries[:, low:high]
        g_block = grads[:, low:high]
        q_back = q_block.T
        g_back = g_block.T
        mixed_parts = []
        dq_parts = []
        for at in range(width // head):
            rows = slice(at * head, (at + 1) * head)
            mine = row_of == at
            q_own = jnp.where(mine, q_block, jnp.bfloat16(0))
            g_own = jnp.where(mine, g_block, jnp.bfloat16(0))
            scores = nn(keys_t[:high], q_own)
            scores = jnp.where(allowed, scores, MASKED)
            top = jnp.max(scores, axis=0, keepdims=True)
            weights = jnp.exp(scores - top)
            weights = weights * (1.0 / jnp.sum(weights, axis=0, keepdims=True))
            weights_low = weights.astype(jnp.bfloat16)
            mixed_parts.append(nn(values[rows, :high], weights_low))
            dweights = nn(values_t[:high], g_own)
            delta = jnp.sum(weights * dweights, axis=0, keepdims=True)
            dscores = (weights * (dweights - delta)).astype(jnp.bfloat16)
            dq_parts.append(nn(keys[rows, :high], dscores))
            own_lane = lane_of == at
            dk_ref[:high, :] += nn(dscores, jnp.where(own_lane, q_back, jnp.bfloat16(0)))
            dv_ref[:high, :] += nn(weights_low, jnp.where(own_lane, g_back, jnp.bfloat16(0)))
        mixed_ref[:, low:high] = jnp.concatenate(mixed_parts, axis=0).astype(jnp.bfloat16)
        dq = jnp.concatenate(dq_parts, axis=0) * (1.0 / math.sqrt(head))
        grad_ref[0, :, low:high] = turn(dq, cosines[:, low:high], -sines[:, low:high], head).astype(jnp.bfloat16)
    grad_ref[1] = turn(dk_ref[...].T, cosines, -sines, head).astype(jnp.bfloat16)
    grad_ref[2] = dv_ref[...].T.astype(jnp.bfloat16)


def attention(projected_t, dmixed_t, cosines, sines, seq_start, block=512):
    model, count = dmixed_t.shape
    head = model // HEADS
    width = 2 * head
    steps = model // width
    block = min(block, count)
    return pl.pallas_call(
        functools.partial(attention_kernel, block, head),
        grid=(steps,),
        in_specs=[
            pl.BlockSpec((width, count), lambda i: (i, 0)),
            pl.BlockSpec((width, count), lambda i: (i + steps, 0)),
            pl.BlockSpec((width, count), lambda i: (i + 2 * steps, 0)),
            pl.BlockSpec((width, count), lambda i: (i, 0)),
            pl.BlockSpec((ROT // 2, count), lambda i: (0, 0)),
            pl.BlockSpec((ROT // 2, count), lambda i: (0, 0)),
            pl.BlockSpec((1, count), lambda i: (0, 0)),
        ],
        out_specs=[
            pl.BlockSpec((width, count), lambda i: (i, 0)),
            pl.BlockSpec((3, width, count), lambda i: (0, i, 0)),
        ],
        out_shape=[
            jax.ShapeDtypeStruct((model, count), jnp.bfloat16),
            jax.ShapeDtypeStruct((3, model, count), jnp.bfloat16),
        ],
        scratch_shapes=[pltpu.VMEM((count, width), jnp.float32), pltpu.VMEM((count, width), jnp.float32)],
        compiler_params=pltpu.CompilerParams(vmem_limit_bytes=VMEM_LIMIT),
        cost_estimate=pl.CostEstimate(
            flops=12 * count * count * model,
            bytes_accessed=22 * count * model,
            transcendentals=count * count * HEADS // 2,
        ),
        name="attention",
    )(projected_t, projected_t, projected_t, dmixed_t, cosines, sines, seq_start)


def link_bits(count):
    size = count.bit_length() - 1
    top = list(range(size - 1, 2, -1))
    if size < 3:
        return [list(range(size - 1, 0, -1))] * 2
    return [[1] + top + [2], [2] + top + [1]]


def relative_blocks(count):
    by_core = link_bits(count)
    half = count // 2
    tables = []
    for core in range(2):
        places = []
        for place in range(count):
            other = place // half
            bits = by_core[core ^ other]
            distance = other
            for at, bit in enumerate(bits):
                if (place >> (len(bits) - 1 - at)) & 1:
                    distance |= 1 << bit
            places.append(distance)
        tables.append(places)
    return tables


def core_pairs(count):
    return [(i, i ^ 1) for i in range(count)]


def link_pairs(count, axis):
    by_core = link_bits(count)
    return [(i, i ^ (1 << by_core[i & 1][axis])) for i in range(count)]


class Halving:
    def __init__(self, count, blocks):
        self.count = count
        self.sent, self.kept = blocks[count // 4 :], blocks
        self.order = link_order(count)

    def step(self, *fences):
        got = lax.ppermute(self.sent, "dp", link_pairs(self.count, self.order.pop(0)))
        if self.order:
            self.sent, self.kept = combine(self.kept, got, fences)
        else:
            self.kept = self.kept[0].astype(jnp.float32) + got[0].astype(jnp.float32)

    def finish(self):
        while self.order:
            self.step()
        return self.kept


def halve_exactly(count, blocks):
    size = count.bit_length() - 2
    buf = blocks.reshape((2,) * size + blocks.shape[1:])
    for at, stage in enumerate(link_order(count)):
        axis = 0 if at == 0 else size - at - 1
        kept = lax.index_in_dim(buf, 0, axis, keepdims=False)
        sent = lax.index_in_dim(buf, 1, axis, keepdims=False)
        buf = kept + lax.ppermute(sent, "dp", link_pairs(count, stage))
    return buf


def link_order(count):
    size = count.bit_length() - 2
    return [0] + list(range(size - 1, 0, -1))


def collect(count, own):
    size = count.bit_length() - 2
    buf = own.reshape((1,) * size + own.shape)
    for stage in link_order(count)[::-1]:
        got = lax.ppermute(buf, "dp", link_pairs(count, stage))
        buf = jnp.concatenate([buf, got], axis=stage)
    low = buf.reshape((count // 2,) + own.shape)
    return low, lax.ppermute(low, "dp", core_pairs(count))


def nothing(*values):
    total = 0.0
    for value in values:
        total = total + value[(0,) * value.ndim].astype(jnp.float32) * 0.0
    return total


def later(shard, *values):
    return (shard.astype(jnp.float32) + nothing(*values)).astype(shard.dtype)


def tn(a, b):
    return lax.dot_general(a, b, (((0,), (0,)), ((), ())), preferred_element_type=jnp.float32)


def tn_pair(a, b):
    return lax.dot_general(a, b, (((1,), (0,)), ((), ())), preferred_element_type=jnp.float32)


def norm_parts(stream):
    row_mean = jnp.mean(stream, axis=-1, keepdims=True)
    centered = stream - row_mean
    spread = jnp.mean(centered * centered, axis=-1, keepdims=True)
    factor = lax.rsqrt(spread + EPSILON)
    return centered * factor, factor


def shards(
    tokens,
    ln1_gain,
    ln1_bias,
    ln2_gain,
    ln2_bias,
    w_qkv,
    b_qkv,
    w_dense,
    b_dense,
    w_up,
    b_up,
    w_down,
    b_down,
    grad_out,
    seq_lengths,
    count,
):
    f32 = jnp.float32
    bf16 = jnp.bfloat16
    rows, model = tokens.shape
    depth = w_up.shape[0]
    own_hidden = w_down.shape[0]
    hidden = count * own_hidden
    me = lax.axis_index("dp").astype(jnp.int32)
    small = [ln1_gain, ln1_bias, ln2_gain, ln2_bias, b_qkv, b_dense, b_up, b_down]
    lanes = 128 * (-(-max(v.shape[0] for v in small) // 128))
    small_rows = jnp.stack([jnp.pad(v, (0, lanes - v.shape[0])) for v in small])
    tables = jnp.asarray(relative_blocks(count), jnp.int32)
    block_at = me ^ tables[me & 1]
    small_low, small_high = collect(count, small_rows)
    smalls = jnp.concatenate([small_low, small_high], axis=0)
    back = jnp.argsort(block_at)
    smalls = jnp.take(smalls, back, axis=0).astype(f32)
    gain1, bias1, gain2, bias2, qkv_b, dense_b, up_b, down_b = (
        smalls[:, at, : v.shape[0]].reshape(1, count * v.shape[0]) for at, v in enumerate(small)
    )
    attention_w = lax.all_gather(jnp.concatenate([w_qkv, w_dense], axis=1), "dp", axis=0, tiled=True)
    qkv_w, dense_w = attention_w[:, : 3 * model], attention_w[:, 3 * model :]

    seq_ends = jnp.cumsum(seq_lengths[0])
    places = jnp.arange(rows, dtype=jnp.int32)
    passed = seq_ends[None, :] <= places[:, None]
    seq_start = jnp.max(jnp.where(passed, seq_ends[None, :], 0), axis=1)
    is_valid = places < seq_ends[-1]
    half_rot = ROT // 2
    frequency = ROPE_BASE ** (-(jnp.arange(half_rot, dtype=f32) * (2.0 / ROT)))
    angles = frequency[:, None] * (places - seq_start).astype(f32)[None, :]
    cosines, sines = jnp.cos(angles), jnp.sin(angles)

    stream = tokens.astype(f32)
    normed, factor = norm_parts(stream)
    first_in = (normed * gain1 + bias1).astype(bf16)
    second_in = (normed * gain2 + bias2).astype(bf16)
    grad_y = grad_out * is_valid.astype(bf16)[:, None]

    row_at = (block_at[:, None] * depth + jnp.arange(depth, dtype=jnp.int32)[None, :]).reshape(model, 1)
    place = (row_at == jnp.arange(model, dtype=jnp.int32)[None, :]).astype(bf16)
    out_bias = jnp.sum(grad_y.astype(f32), axis=0)
    first_t = nt(place, first_in).astype(bf16)
    second_t = nt(place, second_in).astype(bf16)

    grouped = own_hidden % 128 == 0 and count >= 8 and (8 * own_hidden) == model and own_hidden % depth == 0
    if grouped:
        pieces = hidden // model
        stacked_w = jnp.concatenate(
            [w_up[:, at * model : (at + 1) * model] for at in range(pieces)] + [w_down], axis=0
        )
        feed_w = lax.all_gather(later(stacked_w, attention_w, first_t, second_t, cosines, sines, out_bias), "dp", axis=0, tiled=True)
        feed_w = feed_w.reshape(count, -1, depth, model)
    else:
        up_w = lax.all_gather(later(w_up, attention_w), "dp", axis=0, tiled=True)
        down_w = lax.all_gather(later(w_down, up_w), "dp", axis=0, tiled=True)

    def exchange(upper, lower, rhs, rule, *fences):
        sent = (rule(upper, rhs) + nothing(*fences)).astype(bf16)
        got = lax.ppermute(sent, "dp", core_pairs(count))
        kept = (rule(lower, rhs) + got.astype(f32)).astype(bf16)
        return kept.reshape(count // 2, -1, kept.shape[-1])

    half = model // 2
    projected_t = lax.dot_general(qkv_w, first_in, (((0,), (1,)), ((), ())), preferred_element_type=f32)
    projected_t = projected_t + qkv_b.reshape(-1, 1)
    dmixed_t = nt(dense_w, grad_y).astype(bf16)
    mixed_t, grads_t = attention(projected_t, dmixed_t, cosines, sines, seq_start.reshape(1, rows))
    grads_t = grads_t.reshape(3 * model, rows)
    mixed_p = nn(place, mixed_t).astype(bf16)
    qkv_kept = exchange(first_t[half:], first_t[:half], grads_t, nt)
    dense_kept = exchange(mixed_p[half:], mixed_p[:half], grad_y, nn)
    attention_sum = Halving(count, jnp.concatenate([qkv_kept, dense_kept], axis=-1))
    grad_first = lax.dot_general(grads_t, qkv_w, (((0,), (1,)), ((), ())), preferred_element_type=f32)
    attention_out = lax.dot_general(mixed_t, dense_w, (((0,), (0,)), ((), ())), preferred_element_type=f32)
    if grouped:
        act, act_halves, dpre, up_sums = feed_forward(
            me.reshape(1), second_in, grad_y, feed_w, up_b, own_hidden, (attention_sum.sent, grad_first, attention_out)
        )
    else:
        act, slope = gelu_pair(nn(second_in, up_w) + up_b)
        act = act.astype(bf16)
        act_p = jnp.take(act.reshape(rows, count, own_hidden), block_at, axis=1).reshape(rows, hidden)
        act_halves = jnp.stack(jnp.split(act_p, 4, axis=1)).reshape(2, 2, rows, hidden // 4)
        dpre = (nt(grad_y, down_w) * slope).astype(bf16)
        up_sums = jnp.sum(dpre.astype(f32), axis=0)
    attention_sum.step(dpre)
    down_sum = Halving(count, exchange(act_halves[1], act_halves[0], grad_y, tn_pair, attention_sum.kept))
    up_sum = Halving(count, exchange(second_t[half:], second_t[:half], dpre, nn))
    attention_sum.step(up_sum.kept)
    down_sum.step(up_sum.kept)

    if grouped:
        after = (up_sum.sent, down_sum.sent)
        grad_second = feed_close(dpre, feed_w, own_hidden, nt, after)
    else:
        grad_second = nt(dpre, up_w)
    small_grads = [
        jnp.sum(grad_first * normed, axis=0),
        jnp.sum(grad_first, axis=0),
        jnp.sum(grad_second * normed, axis=0),
        jnp.sum(grad_second, axis=0),
        jnp.sum(grads_t.astype(f32), axis=1),
        out_bias,
        up_sums.reshape(-1),
    ]
    down_sum.step(grad_second)
    up_sum.step(grad_second, small_grads[2], small_grads[3])
    if attention_sum.order:
        attention_sum.step(grad_second)
    attention_part = attention_sum.finish()
    qkv_part, dense_part = attention_part[:, : 3 * model], attention_part[:, 3 * model :]
    pull = grad_first * gain1 + grad_second * gain2
    pull_mean = jnp.mean(pull, axis=-1, keepdims=True)
    pull_norm = jnp.mean(pull * normed, axis=-1, keepdims=True)
    grad_x = factor * (pull - pull_mean - normed * pull_norm)
    grad_tokens = (grad_y.astype(f32) + grad_x).astype(bf16)
    if grouped:
        feed_out = feed_close(act, feed_w, own_hidden, nn, (down_sum.sent, up_sum.sent))
    else:
        feed_out = nn(act, down_w)
    down_sum.step(feed_out)
    up_sum.step(feed_out)
    if up_sum.order:
        up_sum.step(grad_tokens)
    down_part = down_sum.finish()
    stacked = jnp.concatenate([v.reshape(count, -1) for v in small_grads], axis=1)
    stacked = jnp.take(stacked, block_at, axis=0) + nothing(up_sum.kept, down_part, attention_part)
    middle = count // 2
    buf = stacked[:middle] + lax.ppermute(stacked[middle:], "dp", core_pairs(count))
    result = (stream + attention_out + dense_b + feed_out + down_b).astype(bf16)
    up_part = up_sum.finish()
    buf = halve_exactly(count, buf.reshape(middle, 1, -1))
    small_out = []
    at = 0
    for v in small_grads:
        size = v.shape[0] // count
        small_out.append(buf[0, at : at + size])
        at += size
    gain1_part, bias1_part, gain2_part, bias2_part, qkv_bias_part, out_bias_part, up_bias_part = small_out
    return (
        result,
        grad_tokens,
        gain1_part,
        bias1_part,
        gain2_part,
        bias2_part,
        qkv_part,
        qkv_bias_part,
        dense_part,
        out_bias_part,
        up_part,
        up_bias_part,
        down_part,
        out_bias_part,
    )


def solution(mesh):
    count = mesh.shape["dp"]
    row, flat = P("dp", None), P("dp")
    in_specs = (row, flat, flat, flat, flat, row, flat, row, flat, row, flat, row, flat, row, row)
    out_specs = (row, row, flat, flat, flat, flat, row, flat, row, flat, row, flat, row, flat)
    return jax.shard_map(
        functools.partial(shards, count=count), mesh=mesh, in_specs=in_specs, out_specs=out_specs, check_vma=False
    )
```

```python
import functools
import math

import jax
import jax.numpy as jnp
from jax import lax
from jax.experimental import pallas as pl
from jax.experimental.pallas import tpu as pltpu
from jax.sharding import PartitionSpec as P

HEADS = 16
ROT = 16
EPSILON = 1e-05
ROPE_BASE = 10000.0
MASKED = -1e30
VMEM_LIMIT = 56 * 1024 * 1024

ERF_P = 0.38
ERF_C = (
    0.2144098448037192,
    0.21394421331748759,
    0.20368721918248728,
    0.13967175645997887,
    0.22724170102679003,
    -0.15687572740913802,
    0.3593738707984917,
    -0.25987872992383027,
    0.05842583978543742,
)


def gelu_pair(pre):
    size = jnp.abs(pre)
    bell = jnp.exp(pre * pre * -0.5)
    t = pltpu.reciprocal(size * (ERF_P / math.sqrt(2.0)) + 1.0, approx=False)
    poly = jnp.full_like(t, 0.5 * ERF_C[-1])
    for coef in ERF_C[-2::-1]:
        poly = poly * t + 0.5 * coef
    tail = poly * t * bell
    cdf = jnp.where(pre < 0.0, tail, 1.0 - tail)
    return pre * cdf, cdf + pre * bell * (1.0 / math.sqrt(2.0 * math.pi))


def nt(a, b):
    return lax.dot_general(a, b, (((1,), (1,)), ((), ())), preferred_element_type=jnp.float32)


def nn(a, b):
    return jnp.dot(a, b, preferred_element_type=jnp.float32)


def feed_kernel(rows, own, me_ref, h_ref, dy_ref, up_ref, bias_ref, down_ref, *refs):
    act_ref, halves_ref, dpre_ref, dbias_ref = refs[-4:]
    total, model = h_ref.shape
    block = 8 * own
    up = up_ref[...].reshape(model, block)
    down = down_ref[...].reshape(block, model)
    me = me_ref[0]
    core = me & 1
    spots = []
    for x in range(2):
        for y in range(2):
            far_x = ((me >> 1) & 1) ^ x
            far_y = ((me >> 2) & 1) ^ y
            x_lane = pl.ds(pl.multiple_of(far_x * own, own), own)
            y_lane = pl.ds(pl.multiple_of(far_y * own, own), own)
            spots.append(((y * 4 + x * 2) * own, far_x, x_lane, far_y, y_lane))
    sums = jnp.zeros((1, block), jnp.float32)
    for start in range(0, total, rows):
        part = pl.ds(start, rows)
        pre = nn(h_ref[part, :], up) + bias_ref[...]
        dact = nt(dy_ref[part, :], down)
        act, slope = gelu_pair(pre)
        act = act.astype(jnp.bfloat16)
        act_ref[part, :] = act
        dpre = (dact * slope).astype(jnp.bfloat16)
        dpre_ref[part, :] = dpre
        sums = sums + jnp.sum(dpre.astype(jnp.float32), axis=0, keepdims=True)
        for at, far_x, x_lane, far_y, y_lane in spots:
            halves_ref[core, far_x, part, y_lane] = act[:, at : at + own]
            halves_ref[1 - core, far_y, part, x_lane] = act[:, at + own : at + 2 * own]
    dbias_ref[...] = sums


def feed_specs(count, model, own, depth, devices):
    pieces = 8 * own // model
    up = pl.BlockSpec((devices, pieces, depth, model), lambda i, *me: (0, i, 0, 0))
    span = own // depth
    down = pl.BlockSpec((8, span, depth, model), lambda i, *me: (i, 1, 0, 0))
    return up, down


def feed_forward(me, h, dy, weights, bias, own, after, rows=512):
    count, model = h.shape
    devices, depth = weights.shape[0], weights.shape[2]
    hidden = devices * own
    block = 8 * own
    whole = pl.BlockSpec((count, model), lambda i, me: (0, 0))
    wide = pl.BlockSpec((count, block), lambda i, me: (0, i))
    halves = pl.BlockSpec((2, 2, count, block // 4), lambda i, me: (0, 0, 0, i ^ (me[0] >> 3)))
    line = pl.BlockSpec((1, block), lambda i, me: (0, i))
    whole_shape = jax.ShapeDtypeStruct((count, hidden), jnp.bfloat16)
    halves_shape = jax.ShapeDtypeStruct((2, 2, count, hidden // 4), jnp.bfloat16)
    up, down = feed_specs(count, model, own, depth, devices)
    return pl.pallas_call(
        functools.partial(feed_kernel, min(rows, count), own),
        grid_spec=pltpu.PrefetchScalarGridSpec(
            num_scalar_prefetch=1,
            grid=(hidden // block,),
            in_specs=[whole, whole, up, line, down] + [pl.BlockSpec(memory_space=pl.ANY)] * len(after),
            out_specs=[wide, halves, wide, line],
        ),
        out_shape=[whole_shape, halves_shape, whole_shape, jax.ShapeDtypeStruct((1, hidden), jnp.float32)],
        compiler_params=pltpu.CompilerParams(vmem_limit_bytes=VMEM_LIMIT),
        cost_estimate=pl.CostEstimate(
            flops=4 * count * model * hidden,
            bytes_accessed=4 * count * model + 4 * model * hidden + 6 * count * hidden,
            transcendentals=2 * count * hidden,
        ),
        name="feed_forward",
    )(me, h, dy, weights, bias, weights, *after)


def close_kernel(rows, own, rule, left_ref, right_ref, *refs):
    out_ref = refs[-1]
    total, model = out_ref.shape
    block = 8 * own
    right = right_ref[...].reshape((model, block) if rule is nt else (block, model))

    @pl.when(pl.program_id(0) == 0)
    def _():
        out_ref[...] = jnp.zeros_like(out_ref)

    for start in range(0, total, rows):
        part = pl.ds(start, rows)
        out_ref[part, :] += rule(left_ref[part, :], right)


def feed_close(left, weights, own, rule, after, rows=512):
    count, hidden = left.shape
    devices, depth, model = weights.shape[0], weights.shape[2], weights.shape[3]
    wide = pl.BlockSpec((count, 8 * own), lambda i: (0, i))
    whole = pl.BlockSpec((count, model), lambda i: (0, 0))
    up, down = feed_specs(count, model, own, depth, devices)
    return pl.pallas_call(
        functools.partial(close_kernel, min(rows, count), own, rule),
        grid=(hidden // (8 * own),),
        in_specs=[wide, up if rule is nt else down] + [pl.BlockSpec(memory_space=pl.ANY)] * len(after),
        out_specs=whole,
        out_shape=jax.ShapeDtypeStruct((count, model), jnp.float32),
        compiler_params=pltpu.CompilerParams(vmem_limit_bytes=VMEM_LIMIT),
        cost_estimate=pl.CostEstimate(
            flops=2 * count * model * hidden,
            bytes_accessed=4 * count * model + 2 * model * hidden + 2 * count * hidden,
            transcendentals=0,
        ),
        name="feed_close",
    )(left, weights, *after)


def combine_kernel(kept_ref, got_ref, *refs):
    sent_ref, left_ref = refs[-2:]
    total = kept_ref[0].astype(jnp.float32) + got_ref[0].astype(jnp.float32)
    total = total.astype(jnp.bfloat16)
    left_ref[0] = total[0]
    sent_ref[0] = total[1]


def combine(kept, got, after):
    places, rows, columns = got.shape
    pair = pl.BlockSpec((1, 2, rows, columns), lambda i: (i, 0, 0, 0))
    one = pl.BlockSpec((1, rows, columns), lambda i: (i, 0, 0))
    shape = jax.ShapeDtypeStruct((places // 2, rows, columns), jnp.bfloat16)
    paired = (-1, 2, rows, columns)
    return pl.pallas_call(
        combine_kernel,
        grid=(places // 2,),
        in_specs=[pair, pair] + [pl.BlockSpec(memory_space=pl.ANY)] * len(after),
        out_specs=[one, one],
        out_shape=[shape, shape],
        compiler_params=pltpu.CompilerParams(vmem_limit_bytes=VMEM_LIMIT),
        cost_estimate=pl.CostEstimate(
            flops=places * rows * columns, bytes_accessed=6 * places * rows * columns, transcendentals=0
        ),
        name="combine",
    )(kept.reshape(paired), got.reshape(paired), *after)


def turn(x, cosines, sines, head):
    half = ROT // 2
    parts = []
    for start in range(0, x.shape[0], head):
        first = x[start : start + half]
        second = x[start + half : start + ROT]
        parts.append(first * cosines - second * sines)
        parts.append(second * cosines + first * sines)
        parts.append(x[start + ROT : start + head])
    return jnp.concatenate(parts, axis=0)


def attention_kernel(
    block, head, q_ref, k_ref, v_ref, g_ref, cos_ref, sin_ref, start_ref, mixed_ref, grad_ref, dk_ref, dv_ref
):
    width, count = q_ref.shape
    cosines = cos_ref[...]
    sines = sin_ref[...]
    queries = turn(q_ref[...], cosines, sines, head).astype(jnp.bfloat16) * jnp.bfloat16(1.0 / math.sqrt(head))
    keys = turn(k_ref[...], cosines, sines, head).astype(jnp.bfloat16)
    values = v_ref[...].astype(jnp.bfloat16)
    grads = g_ref[...]
    keys_t = keys.T
    values_t = values.T
    row_of = lax.broadcasted_iota(jnp.int32, (width, 1), 0) // head
    lane_of = lax.broadcasted_iota(jnp.int32, (1, width), 1) // head
    dk_ref[...] = jnp.zeros_like(dk_ref)
    dv_ref[...] = jnp.zeros_like(dv_ref)
    for low in range(0, count, block):
        high = low + block
        seq_start = start_ref[:, low:high]
        key_at = lax.broadcasted_iota(jnp.int32, (high, block), 0)
        query_at = lax.broadcasted_iota(jnp.int32, (high, block), 1) + low
        allowed = (key_at >= seq_start) & (key_at <= query_at)
        q_block = queries[:, low:high]
        g_block = grads[:, low:high]
        q_back = q_block.T
        g_back = g_block.T
        mixed_parts = []
        dq_parts = []
        for at in range(width // head):
            rows = slice(at * head, (at + 1) * head)
            mine = row_of == at
            q_own = jnp.where(mine, q_block, jnp.bfloat16(0))
            g_own = jnp.where(mine, g_block, jnp.bfloat16(0))
            scores = nn(keys_t[:high], q_own)
            scores = jnp.where(allowed, scores, MASKED)
            top = jnp.max(scores, axis=0, keepdims=True)
            weights = jnp.exp(scores - top)
            weights = weights * (1.0 / jnp.sum(weights, axis=0, keepdims=True))
            weights_low = weights.astype(jnp.bfloat16)
            mixed_parts.append(nn(values[rows, :high], weights_low))
            dweights = nn(values_t[:high], g_own)
            delta = jnp.sum(weights * dweights, axis=0, keepdims=True)
            dscores = (weights * (dweights - delta)).astype(jnp.bfloat16)
            dq_parts.append(nn(keys[rows, :high], dscores))
            own_lane = lane_of == at
            dk_ref[:high, :] += nn(dscores, jnp.where(own_lane, q_back, jnp.bfloat16(0)))
            dv_ref[:high, :] += nn(weights_low, jnp.where(own_lane, g_back, jnp.bfloat16(0)))
        mixed_ref[:, low:high] = jnp.concatenate(mixed_parts, axis=0).astype(jnp.bfloat16)
        dq = jnp.concatenate(dq_parts, axis=0) * (1.0 / math.sqrt(head))
        grad_ref[0, :, low:high] = turn(dq, cosines[:, low:high], -sines[:, low:high], head).astype(jnp.bfloat16)
    grad_ref[1] = turn(dk_ref[...].T, cosines, -sines, head).astype(jnp.bfloat16)
    grad_ref[2] = dv_ref[...].T.astype(jnp.bfloat16)


def attention(projected_t, dmixed_t, cosines, sines, seq_start, block=512):
    model, count = dmixed_t.shape
    head = model // HEADS
    width = 2 * head
    steps = model // width
    block = min(block, count)
    return pl.pallas_call(
        functools.partial(attention_kernel, block, head),
        grid=(steps,),
        in_specs=[
            pl.BlockSpec((width, count), lambda i: (i, 0)),
            pl.BlockSpec((width, count), lambda i: (i + steps, 0)),
            pl.BlockSpec((width, count), lambda i: (i + 2 * steps, 0)),
            pl.BlockSpec((width, count), lambda i: (i, 0)),
            pl.BlockSpec((ROT // 2, count), lambda i: (0, 0)),
            pl.BlockSpec((ROT // 2, count), lambda i: (0, 0)),
            pl.BlockSpec((1, count), lambda i: (0, 0)),
        ],
        out_specs=[
            pl.BlockSpec((width, count), lambda i: (i, 0)),
            pl.BlockSpec((3, width, count), lambda i: (0, i, 0)),
        ],
        out_shape=[
            jax.ShapeDtypeStruct((model, count), jnp.bfloat16),
            jax.ShapeDtypeStruct((3, model, count), jnp.bfloat16),
        ],
        scratch_shapes=[pltpu.VMEM((count, width), jnp.float32), pltpu.VMEM((count, width), jnp.float32)],
        compiler_params=pltpu.CompilerParams(vmem_limit_bytes=VMEM_LIMIT),
        cost_estimate=pl.CostEstimate(
            flops=12 * count * count * model,
            bytes_accessed=22 * count * model,
            transcendentals=count * count * HEADS // 2,
        ),
        name="attention",
    )(projected_t, projected_t, projected_t, dmixed_t, cosines, sines, seq_start)


def link_bits(count):
    size = count.bit_length() - 1
    top = list(range(size - 1, 2, -1))
    if size < 3:
        return [list(range(size - 1, 0, -1))] * 2
    return [[1] + top + [2], [2] + top + [1]]


def relative_blocks(count):
    by_core = link_bits(count)
    half = count // 2
    tables = []
    for core in range(2):
        places = []
        for place in range(count):
            other = place // half
            bits = by_core[core ^ other]
            distance = other
            for at, bit in enumerate(bits):
                if (place >> (len(bits) - 1 - at)) & 1:
                    distance |= 1 << bit
            places.append(distance)
        tables.append(places)
    return tables


def core_pairs(count):
    return [(i, i ^ 1) for i in range(count)]


def link_pairs(count, axis):
    by_core = link_bits(count)
    return [(i, i ^ (1 << by_core[i & 1][axis])) for i in range(count)]


class Halving:
    def __init__(self, count, blocks):
        self.count = count
        self.sent, self.kept = blocks[count // 4 :], blocks
        self.order = link_order(count)

    def step(self, *fences):
        got = lax.ppermute(self.sent, "dp", link_pairs(self.count, self.order.pop(0)))
        if self.order:
            self.sent, self.kept = combine(self.kept, got, fences)
        else:
            self.kept = self.kept[0].astype(jnp.float32) + got[0].astype(jnp.float32)

    def finish(self):
        while self.order:
            self.step()
        return self.kept


def halve_exactly(count, blocks):
    size = count.bit_length() - 2
    buf = blocks.reshape((2,) * size + blocks.shape[1:])
    for at, stage in enumerate(link_order(count)):
        axis = 0 if at == 0 else size - at - 1
        kept = lax.index_in_dim(buf, 0, axis, keepdims=False)
        sent = lax.index_in_dim(buf, 1, axis, keepdims=False)
        buf = kept + lax.ppermute(sent, "dp", link_pairs(count, stage))
    return buf


def link_order(count):
    size = count.bit_length() - 2
    return [0] + list(range(size - 1, 0, -1))


def collect(count, own):
    size = count.bit_length() - 2
    buf = own.reshape((1,) * size + own.shape)
    for stage in link_order(count)[::-1]:
        got = lax.ppermute(buf, "dp", link_pairs(count, stage))
        buf = jnp.concatenate([buf, got], axis=stage)
    low = buf.reshape((count // 2,) + own.shape)
    return low, lax.ppermute(low, "dp", core_pairs(count))


def nothing(*values):
    total = 0.0
    for value in values:
        total = total + value[(0,) * value.ndim].astype(jnp.float32) * 0.0
    return total


def later(shard, *values):
    return (shard.astype(jnp.float32) + nothing(*values)).astype(shard.dtype)


def tn(a, b):
    return lax.dot_general(a, b, (((0,), (0,)), ((), ())), preferred_element_type=jnp.float32)


def tn_pair(a, b):
    return lax.dot_general(a, b, (((1,), (0,)), ((), ())), preferred_element_type=jnp.float32)


def norm_parts(stream):
    row_mean = jnp.mean(stream, axis=-1, keepdims=True)
    centered = stream - row_mean
    spread = jnp.mean(centered * centered, axis=-1, keepdims=True)
    factor = lax.rsqrt(spread + EPSILON)
    return centered * factor, factor


def shards(
    tokens,
    ln1_gain,
    ln1_bias,
    ln2_gain,
    ln2_bias,
    w_qkv,
    b_qkv,
    w_dense,
    b_dense,
    w_up,
    b_up,
    w_down,
    b_down,
    grad_out,
    seq_lengths,
    count,
):
    f32 = jnp.float32
    bf16 = jnp.bfloat16
    rows, model = tokens.shape
    depth = w_up.shape[0]
    own_hidden = w_down.shape[0]
    hidden = count * own_hidden
    me = lax.axis_index("dp").astype(jnp.int32)
    small = [ln1_gain, ln1_bias, ln2_gain, ln2_bias, b_qkv, b_dense, b_up, b_down]
    lanes = 128 * (-(-max(v.shape[0] for v in small) // 128))
    small_rows = jnp.stack([jnp.pad(v, (0, lanes - v.shape[0])) for v in small])
    tables = jnp.asarray(relative_blocks(count), jnp.int32)
    block_at = me ^ tables[me & 1]
    small_low, small_high = collect(count, small_rows)
    smalls = jnp.concatenate([small_low, small_high], axis=0)
    back = jnp.argsort(block_at)
    smalls = jnp.take(smalls, back, axis=0).astype(f32)
    gain1, bias1, gain2, bias2, qkv_b, dense_b, up_b, down_b = (
        smalls[:, at, : v.shape[0]].reshape(1, count * v.shape[0]) for at, v in enumerate(small)
    )
    attention_w = lax.all_gather(jnp.concatenate([w_qkv, w_dense], axis=1), "dp", axis=0, tiled=True)
    qkv_w, dense_w = attention_w[:, : 3 * model], attention_w[:, 3 * model :]

    seq_ends = jnp.cumsum(seq_lengths[0])
    places = jnp.arange(rows, dtype=jnp.int32)
    passed = seq_ends[None, :] <= places[:, None]
    seq_start = jnp.max(jnp.where(passed, seq_ends[None, :], 0), axis=1)
    is_valid = places < seq_ends[-1]
    half_rot = ROT // 2
    frequency = ROPE_BASE ** (-(jnp.arange(half_rot, dtype=f32) * (2.0 / ROT)))
    angles = frequency[:, None] * (places - seq_start).astype(f32)[None, :]
    cosines, sines = jnp.cos(angles), jnp.sin(angles)

    stream = tokens.astype(f32)
    normed, factor = norm_parts(stream)
    first_in = (normed * gain1 + bias1).astype(bf16)
    second_in = (normed * gain2 + bias2).astype(bf16)
    grad_y = grad_out * is_valid.astype(bf16)[:, None]

    row_at = (block_at[:, None] * depth + jnp.arange(depth, dtype=jnp.int32)[None, :]).reshape(model, 1)
    place = (row_at == jnp.arange(model, dtype=jnp.int32)[None, :]).astype(bf16)
    out_bias = jnp.sum(grad_y.astype(f32), axis=0)
    first_t = nt(place, first_in).astype(bf16)
    second_t = nt(place, second_in).astype(bf16)

    grouped = own_hidden % 128 == 0 and count >= 8 and (8 * own_hidden) == model and own_hidden % depth == 0
    if grouped:
        pieces = hidden // model
        stacked_w = jnp.concatenate(
            [w_up[:, at * model : (at + 1) * model] for at in range(pieces)] + [w_down], axis=0
        )
        feed_w = lax.all_gather(later(stacked_w, attention_w, first_t, second_t, cosines, sines, out_bias), "dp", axis=0, tiled=True)
        feed_w = feed_w.reshape(count, -1, depth, model)
    else:
        up_w = lax.all_gather(later(w_up, attention_w), "dp", axis=0, tiled=True)
        down_w = lax.all_gather(later(w_down, up_w), "dp", axis=0, tiled=True)

    def exchange(upper, lower, rhs, rule, *fences):
        sent = (rule(upper, rhs) + nothing(*fences)).astype(bf16)
        got = lax.ppermute(sent, "dp", core_pairs(count))
        kept = (rule(lower, rhs) + got.astype(f32)).astype(bf16)
        return kept.reshape(count // 2, -1, kept.shape[-1])

    half = model // 2
    projected_t = lax.dot_general(qkv_w, first_in, (((0,), (1,)), ((), ())), preferred_element_type=f32)
    projected_t = projected_t + qkv_b.reshape(-1, 1)
    dmixed_t = nt(dense_w, grad_y).astype(bf16)
    mixed_t, grads_t = attention(projected_t, dmixed_t, cosines, sines, seq_start.reshape(1, rows))
    grads_t = grads_t.reshape(3 * model, rows)
    mixed_p = nn(place, mixed_t).astype(bf16)
    qkv_kept = exchange(first_t[half:], first_t[:half], grads_t, nt)
    dense_kept = exchange(mixed_p[half:], mixed_p[:half], grad_y, nn)
    attention_sum = Halving(count, jnp.concatenate([qkv_kept, dense_kept], axis=-1))
    grad_first = lax.dot_general(grads_t, qkv_w, (((0,), (1,)), ((), ())), preferred_element_type=f32)
    attention_out = lax.dot_general(mixed_t, dense_w, (((0,), (0,)), ((), ())), preferred_element_type=f32)
    if grouped:
        act, act_halves, dpre, up_sums = feed_forward(
            me.reshape(1), second_in, grad_y, feed_w, up_b, own_hidden, (attention_sum.sent, grad_first, attention_out)
        )
    else:
        act, slope = gelu_pair(nn(second_in, up_w) + up_b)
        act = act.astype(bf16)
        act_p = jnp.take(act.reshape(rows, count, own_hidden), block_at, axis=1).reshape(rows, hidden)
        act_halves = jnp.stack(jnp.split(act_p, 4, axis=1)).reshape(2, 2, rows, hidden // 4)
        dpre = (nt(grad_y, down_w) * slope).astype(bf16)
        up_sums = jnp.sum(dpre.astype(f32), axis=0)
    attention_sum.step(dpre)
    down_sum = Halving(count, exchange(act_halves[1], act_halves[0], grad_y, tn_pair, attention_sum.kept))
    up_sum = Halving(count, exchange(second_t[half:], second_t[:half], dpre, nn))
    attention_sum.step(up_sum.kept)
    down_sum.step(up_sum.kept)

    if grouped:
        after = (up_sum.sent, down_sum.sent)
        grad_second = feed_close(dpre, feed_w, own_hidden, nt, after)
    else:
        grad_second = nt(dpre, up_w)
    small_grads = [
        jnp.sum(grad_first * normed, axis=0),
        jnp.sum(grad_first, axis=0),
        jnp.sum(grad_second * normed, axis=0),
        jnp.sum(grad_second, axis=0),
        jnp.sum(grads_t.astype(f32), axis=1),
        out_bias,
        up_sums.reshape(-1),
    ]
    down_sum.step(grad_second)
    up_sum.step(grad_second, small_grads[2], small_grads[3])
    if attention_sum.order:
        attention_sum.step(grad_second)
    attention_part = attention_sum.finish()
    qkv_part, dense_part = attention_part[:, : 3 * model], attention_part[:, 3 * model :]
    pull = grad_first * gain1 + grad_second * gain2
    pull_mean = jnp.mean(pull, axis=-1, keepdims=True)
    pull_norm = jnp.mean(pull * normed, axis=-1, keepdims=True)
    grad_x = factor * (pull - pull_mean - normed * pull_norm)
    grad_tokens = (grad_y.astype(f32) + grad_x).astype(bf16)
    if grouped:
        feed_out = feed_close(act, feed_w, own_hidden, nn, (down_sum.sent, up_sum.sent))
    else:
        feed_out = nn(act, down_w)
    down_sum.step(feed_out)
    up_sum.step(feed_out)
    if up_sum.order:
        up_sum.step(grad_tokens)
    down_part = down_sum.finish()
    stacked = jnp.concatenate([v.reshape(count, -1) for v in small_grads], axis=1)
    stacked = jnp.take(stacked, block_at, axis=0) + nothing(up_sum.kept, down_part, attention_part)
    middle = count // 2
    buf = stacked[:middle] + lax.ppermute(stacked[middle:], "dp", core_pairs(count))
    result = (stream + attention_out + dense_b + feed_out + down_b).astype(bf16)
    up_part = up_sum.finish()
    buf = halve_exactly(count, buf.reshape(middle, 1, -1))
    small_out = []
    at = 0
    for v in small_grads:
        size = v.shape[0] // count
        small_out.append(buf[0, at : at + size])
        at += size
    gain1_part, bias1_part, gain2_part, bias2_part, qkv_bias_part, out_bias_part, up_bias_part = small_out
    return (
        result,
        grad_tokens,
        gain1_part,
        bias1_part,
        gain2_part,
        bias2_part,
        qkv_part,
        qkv_bias_part,
        dense_part,
        out_bias_part,
        up_part,
        up_bias_part,
        down_part,
        out_bias_part,
    )


def solution(mesh):
    count = mesh.shape["dp"]
    row, flat = P("dp", None), P("dp")
    in_specs = (row, flat, flat, flat, flat, row, flat, row, flat, row, flat, row, flat, row, row)
    out_specs = (row, row, flat, flat, flat, flat, row, flat, row, flat, row, flat, row, flat)
    return jax.shard_map(
        functools.partial(shards, count=count), mesh=mesh, in_specs=in_specs, out_specs=out_specs, check_vma=False
    )
```
